32 devices in a mesh: layer: 4 (over x, core), rows: 8 (over z, y).
Axes of the slice: x: 2, y: 2, z: 4, core: 2. Of those that a mesh axis runs over, the one named last changes fastest.
Arguments:
- key_weight: bfloat16 [4, 8192, 512], P('layer', 'rows'), may hold values from -0.0625 to 0.0625
- value_weight: bfloat16 [4, 8192, 512], P('layer', 'rows'), may hold values from -0.0625 to 0.0625
- key_grad: bfloat16 [4, 8192, 512], P('layer', 'rows'), may hold values from -8000 to 8000
- value_grad: bfloat16 [4, 8192, 512], P('layer', 'rows'), may hold values from -8000 to 8000
Outputs:
- key_update: bfloat16 [4, 8192, 512], P('layer', 'rows')
- value_update: bfloat16 [4, 8192, 512], P('layer', 'rows')
- key_dual: float32 [4, 512, 512], P('layer', 'rows')
- value_dual: float32 [4, 512, 512], P('layer', 'rows')
The draws below stay inside these ranges and needn't reach their ends.
All inputs are finite; a program needn't handle non-finite values.
Results may differ from the reference program's by a relative error of at most 0.033.
Values may be sent and summed in bfloat16 or wider, within the bound.
A program may use at most 64 MiB of HBM per device.

```python
import jax
import jax.numpy as jnp
from jax import lax

D = 8192
COLS = 512
DUAL_ITERS = 2
NS_STEPS = 3
LAYERS = 4


def sign_terms(key, strengths):
    result = jnp.zeros((LAYERS, D, COLS), jnp.float32)
    for number, strength in enumerate(strengths):
        row_key, column_key = jax.random.split(jax.random.fold_in(key, number))
        row_sign = jax.random.rademacher(row_key, (LAYERS, D, 1), jnp.float32)
        column_sign = jax.random.rademacher(column_key, (LAYERS, 1, COLS), jnp.float32)
        result = result + strength * row_sign * column_sign
    return result


def grad_draw(key, salt):
    base_key = jax.random.fold_in(key, salt)
    noise_key = jax.random.fold_in(base_key, 0)
    row_key = jax.random.fold_in(base_key, 1)
    column_key = jax.random.fold_in(base_key, 2)
    outer_key = jax.random.fold_in(base_key, 4)
    layer_pos = jnp.arange(LAYERS, dtype=jnp.float32) / max(LAYERS - 1, 1)
    row_pos = jnp.arange(D, dtype=jnp.float32) / (D - 1)
    row_scale = jnp.exp(jax.random.uniform(row_key, (D,), jnp.float32, 0.0, jnp.log(10.0))) * jnp.power(3.0, 0.5 * row_pos)
    column_scale = jnp.exp(jax.random.uniform(column_key, (COLS,), jnp.float32, 0.0, jnp.log(10.0)))
    layer_scale = jnp.power(6.0, layer_pos)
    noise = jnp.clip(jax.random.normal(noise_key, (LAYERS, D, COLS), jnp.float32), -3.0, 3.0)
    noise = noise + sign_terms(outer_key, [2.0, 1.5])
    values = noise * layer_scale[:, None, None] * row_scale[None, :, None] * column_scale[None, None, :]
    return values.astype(jnp.bfloat16)


def draw_key_grad(key, part):
    return grad_draw(key, 11)


def draw_value_grad(key, part):
    return grad_draw(key, 23)


def levels(own_key, shape, cuts, low, top_value):
    loudness = 1.0
    for dim, parts in cuts:
        steps = jax.random.uniform(jax.random.fold_in(jax.random.fold_in(own_key, 6), dim), (parts,), jnp.float32, low / len(cuts), top_value / len(cuts))
        loudness = loudness * jnp.repeat(jnp.exp(steps), shape[dim] // parts).reshape((-1,) + (1,) * (len(shape) - 1 - dim))
    return loudness


def gaussian(own_key, dims, spread, most, pieces=(), kind=jnp.bfloat16):
    values = jax.random.normal(own_key, dims, jnp.float32) * spread
    if len(pieces) > 0:
        values = levels(own_key, dims, pieces, -0.22, 0.18) * values
    return jnp.clip(values, min=-most, max=most).astype(kind)


def setup_inputs(seed: int = 0) -> dict:
    splits = jax.random.split(jax.random.key(seed), 5)
    key_weight = gaussian(splits[0], (LAYERS, D, COLS), D ** -0.5, 0.0625, ((0, 4), (1, 8)))
    value_weight = gaussian(splits[1], (LAYERS, D, COLS), D ** -0.5, 0.0625, ((0, 4), (1, 8)))
    key_grad = draw_key_grad(jax.random.fold_in(splits[4], 71), 0)
    value_grad = draw_value_grad(jax.random.fold_in(splits[4], 71), 0)
    return {"key_weight": key_weight, "value_weight": value_weight, "key_grad": key_grad, "value_grad": value_grad}


first_coeff = 3.4445
third_coeff = -4.775
fifth_coeff = 2.0315
learn_rate = 0.1
dual_rate = 4.0
clip_target = 0.02
epsilon = 1e-06
highest = lax.Precision.HIGHEST

def gram_of(matrix):
    return jnp.dot(matrix.T, matrix, preferred_element_type=jnp.float32)

def make_poly(gram):
    quartic = jnp.dot(gram, gram, precision=highest)
    return (third_coeff * gram + fifth_coeff * quartic).astype(jnp.bfloat16)

def orthogonalize(shifted):
    squares = jnp.sum(jnp.square(shifted.astype(jnp.float32)))
    poly = make_poly(gram_of(shifted) / (squares + epsilon))
    iterate = ((first_coeff * shifted.astype(jnp.float32) + jnp.dot(shifted, poly, preferred_element_type=jnp.float32)) / jnp.sqrt(squares + epsilon)).astype(jnp.bfloat16)
    for repeat in range(NS_STEPS - 1):
        poly = make_poly(gram_of(iterate))
        iterate = (first_coeff * iterate.astype(jnp.float32) + jnp.dot(iterate, poly, preferred_element_type=jnp.float32)).astype(jnp.bfloat16)
    return iterate

def one_matrix(weight, grad, clip):
    dual = jnp.zeros((weight.shape[1], weight.shape[1]), jnp.float32)
    iterate = weight
    for iteration in range(DUAL_ITERS):
        shift = (4.0 * dual).astype(jnp.bfloat16)
        shifted = (clip * grad.astype(jnp.float32) + jnp.dot(weight, shift, preferred_element_type=jnp.float32)).astype(jnp.bfloat16)
        iterate = orthogonalize(shifted)
        cross = jnp.dot(weight.T, iterate, preferred_element_type=jnp.float32)
        dual = dual + dual_rate * -learn_rate * (cross + cross.T)
    update = (-learn_rate * iterate.astype(jnp.float32)).astype(jnp.bfloat16)
    return (update, dual)

def reference(key_weight, value_weight, key_grad, value_grad):
    total = jnp.sum(jnp.square(key_grad.astype(jnp.float32))) + jnp.sum(jnp.square(value_grad.astype(jnp.float32)))
    entries = 2.0 * LAYERS * D * COLS
    clip = clip_target / jnp.sqrt(total / entries + epsilon)

    def per_layer(pair):
        return one_matrix(pair[0], pair[1], clip)
    key_update, key_dual = lax.map(per_layer, (key_weight, key_grad))
    value_update, value_dual = lax.map(per_layer, (value_weight, value_grad))
    return (key_update, value_update, key_dual, value_dual)
```

```python
import functools

import jax
import jax.numpy as jnp
from jax import lax
from jax.experimental import pallas as pl
from jax.experimental.pallas import tpu as pltpu
from jax.sharding import PartitionSpec as P

DUAL_ITERS = 2
NS_STEPS = 3
first_coeff = 3.4445
third_coeff = -4.775
fifth_coeff = 2.0315
learn_rate = 0.1
dual_rate = 4.0
clip_target = 0.02
epsilon = 1e-06

TILE = 128
F32 = jnp.float32
BF16 = jnp.bfloat16
VMEM = pl.BlockSpec(memory_space=pltpu.VMEM)


def block_list(nb):
    upper = [(i, j) for i in range(nb) for j in range(i, nb)]
    return (
        [("A", i, j) for i, j in upper]
        + [("D", i, j) for i, j in upper]
        + [("B", i, j) for i in range(nb) for j in range(nb)]
    )


def strips(nb):
    runs, place = [], 0
    for name in ("A", "D"):
        for i in range(nb):
            runs.append((name, i, i, place))
            place += nb - i
    for i in range(nb):
        runs.append(("B", i, 0, place))
        place += nb
    return runs


def gram_kernel(nb, kw, vw, kg, vg, own, other, tile, gt, wt):
    parity = lax.rem(lax.axis_index("rows"), 2)

    def one(w, g, dst):
        gt[...] = g[...].T
        wt[...] = w[...].T
        for name, i, j, place in strips(nb):
            left = wt if name in ("D", "B") else gt
            right = w if name == "D" else g
            rows = left[i * TILE : (i + 1) * TILE, :]
            value = jnp.dot(rows, right[:, j * TILE :], preferred_element_type=F32).astype(BF16)
            for step in range(nb - j):
                chunk, column = divmod(place + step, nb)
                dst[chunk, :, column * TILE : (column + 1) * TILE] = value[
                    :, step * TILE : (step + 1) * TILE
                ]

    total = jnp.zeros((8, g_cols(kg)), F32)
    rows = kg.shape[0]
    for ref in (kg, vg):
        for start in range(0, rows, 128):
            part = ref[start : start + 128, :].astype(F32)
            total = total + jnp.sum((part * part).reshape(16, 8, -1), axis=0)
    folded = total[:, :TILE]
    for i in range(1, nb):
        folded = folded + total[:, i * TILE : (i + 1) * TILE]
    tile[...] = folded

    @pl.when(parity == 0)
    def _():
        one(vw, vg, other)
        one(kw, kg, own)

    @pl.when(parity == 1)
    def _():
        one(kw, kg, other)
        one(vw, vg, own)


def g_cols(ref):
    return ref.shape[-1]


def reduce_kernel(
    layers, n, own, other, tile, out, total,
    acc, from_pair, from_left, from_right, to_left, to_right,
    layer_tiles, tile_sum, row_tiles,
    pair_sems, left_sems, right_sems, layer_sems, row_sems,
):
    layer = lax.axis_index("layer")
    r = lax.axis_index("rows")
    m = n // 2
    c = r // 2
    pair = r + 1 - 2 * lax.rem(r, 2)
    chunks = own.shape[0]
    MESH = pl.DeviceIdType.MESH

    barrier = pltpu.get_barrier_semaphore()
    for o in range(1, layers):
        peer = (lax.rem(layer + o, layers), r)
        pl.semaphore_signal(barrier, inc=1, device_id=peer, device_id_type=MESH)
    for o in range(1, n):
        peer = (layer, lax.rem(r + o, n))
        pl.semaphore_signal(barrier, inc=1, device_id=peer, device_id_type=MESH)
    pl.semaphore_wait(barrier, layers - 1 + n - 1)

    def layer_copy(o):
        return pltpu.make_async_remote_copy(
            src_ref=tile, dst_ref=layer_tiles.at[o - 1],
            send_sem=layer_sems.at[0, o - 1], recv_sem=layer_sems.at[1, o - 1],
            device_id=(lax.rem(layer + o, layers), r), device_id_type=MESH)

    def row_copy(o):
        return pltpu.make_async_remote_copy(
            src_ref=tile_sum, dst_ref=row_tiles.at[o - 1],
            send_sem=row_sems.at[0, o - 1], recv_sem=row_sems.at[1, o - 1],
            device_id=(layer, lax.rem(r + o, n)), device_id_type=MESH)

    def pair_copy(k):
        return pltpu.make_async_remote_copy(
            src_ref=other.at[k], dst_ref=from_pair.at[k],
            send_sem=pair_sems.at[0, k], recv_sem=pair_sems.at[1, k],
            device_id=(layer, pair), device_id_type=MESH)

    def right_copy(k):
        return pltpu.make_async_remote_copy(
            src_ref=to_right.at[k], dst_ref=from_left.at[k],
            send_sem=right_sems.at[0, k], recv_sem=right_sems.at[1, k],
            device_id=(layer, lax.rem(r + 2, n)), device_id_type=MESH)

    def left_copy(k):
        return pltpu.make_async_remote_copy(
            src_ref=to_left.at[k], dst_ref=from_right.at[k],
            send_sem=left_sems.at[0, k], recv_sem=left_sems.at[1, k],
            device_id=(layer, lax.rem(r + n - 2, n)), device_id_type=MESH)

    for o in range(1, layers):
        layer_copy(o).start()

    def begin(k, carry):
        pair_copy(k).start()
        return carry

    lax.fori_loop(0, chunks, begin, 0)
    for o in range(1, layers):
        layer_copy(o).wait_recv()
    value = tile[...]
    for o in range(1, layers):
        value = value + layer_tiles[o - 1]
    tile_sum[...] = value
    for o in range(1, n):
        row_copy(o).start()

    def step(t, carry):
        @pl.when(t < chunks)
        def _():
            pair_copy(t).wait_recv()
            both = own[t].astype(F32) + from_pair[t].astype(F32)
            acc[t] = both
            out[t] = both

        k = t - c

        @pl.when((k >= 0) & (k < chunks))
        def _():
            @pl.when(c > 0)
            def _():
                right_copy(k).wait_recv()
                out[k] = out[k] + from_left[k].astype(F32)

                @pl.when(c < m - 1)
                def _():
                    to_right[k] = (acc[k] + from_left[k].astype(F32)).astype(BF16)

            @pl.when(c == 0)
            def _():
                to_right[k] = acc[k].astype(BF16)

            @pl.when(c < m - 1)
            def _():
                right_copy(k).start()

        q = t - (m - 1 - c)

        @pl.when((q >= 0) & (q < chunks))
        def _():
            @pl.when(c < m - 1)
            def _():
                left_copy(q).wait_recv()
                out[q] = out[q] + from_right[q].astype(F32)

                @pl.when(c > 0)
                def _():
                    to_left[q] = (acc[q] + from_right[q].astype(F32)).astype(BF16)

            @pl.when(c == m - 1)
            def _():
                to_left[q] = acc[q].astype(BF16)

            @pl.when(c > 0)
            def _():
                left_copy(q).start()

        return carry

    lax.fori_loop(0, chunks + m - 1, step, 0)

    for o in range(1, n):
        row_copy(o).wait_recv()
    value = tile_sum[...]
    for o in range(1, n):
        value = value + row_tiles[o - 1]
    total[...] = value

    def end(k, carry):
        pair_copy(k).wait_send()

        @pl.when(c < m - 1)
        def _():
            right_copy(k).wait_send()

        @pl.when(c > 0)
        def _():
            left_copy(k).wait_send()

        return carry

    lax.fori_loop(0, chunks, end, 0)
    for o in range(1, layers):
        layer_copy(o).wait_send()
    for o in range(1, n):
        row_copy(o).wait_send()


def dual_kernel(nb, n, entries, packed, tile, send, dual, A, B, D, M, Q, T, L, S, F, U, h0, l0, h1, l1):
    size = nb * TILE
    half = size // 2
    r = lax.axis_index("rows")
    clip = clip_target * lax.rsqrt(jnp.full((1, TILE), jnp.sum(tile[...]) / entries + epsilon))
    clip = jnp.max(clip)

    for place, (name, i, j) in enumerate(block_list(nb)):
        chunk, column = divmod(place, nb)
        block = packed[chunk, :, column * TILE : (column + 1) * TILE]
        ref, scale = {"A": (A, clip * clip), "B": (B, clip), "D": (D, None)}[name]
        if scale is not None:
            block = block * scale
        ref[i * TILE : (i + 1) * TILE, j * TILE : (j + 1) * TILE] = block
        if name != "B" and i != j:
            ref[j * TILE : (j + 1) * TILE, i * TILE : (i + 1) * TILE] = block.T

    def split(ref, high, low):
        value = ref[...]
        rounded = value.astype(BF16)
        high[...] = rounded
        low[...] = (value - rounded.astype(F32)).astype(BF16)

    def split_dot(start, xh, xl, yh, yl):
        rows = pl.ds(start, half)
        return (
            jnp.dot(xh[rows, :], yh[...], preferred_element_type=F32)
            + jnp.dot(xh[rows, :], yl[...], preferred_element_type=F32)
            + jnp.dot(xl[rows, :], yh[...], preferred_element_type=F32)
        )

    def multiply(x, y, store):
        split(x, h0, l0)
        same = x is y
        if not same:
            split(y, h1, l1)

        def body(i, carry):
            start = pl.multiple_of(i * half, half)
            store(pl.ds(start, half), split_dot(start, h0, l0, h0 if same else h1, l0 if same else l1))
            return carry

        lax.fori_loop(0, 2, body, 0)

    def eye(rows_start):
        a = lax.broadcasted_iota(jnp.int32, (half, size), 0) + rows_start
        b = lax.broadcasted_iota(jnp.int32, (half, size), 1)
        return a == b

    def put(ref):
        def store(rows, value):
            ref[rows, :] = value
        return store

    def add(ref):
        def store(rows, value):
            ref[rows, :] = ref[rows, :] + value
        return store

    def orthogonalize():
        squares = jnp.float32(0)
        for i in range(2):
            squares = squares + jnp.sum(
                jnp.where(eye(i * half), M[i * half : (i + 1) * half, :], 0.0))
        whole = jnp.full((1, size), squares + epsilon)
        M[...] = M[...] * (1.0 / whole)
        inverse = lax.rsqrt(whole)
        for i in range(2):
            Q[i * half : (i + 1) * half, :] = jnp.where(eye(i * half), inverse, 0.0)

        def ns_step(k, carry):
            def poly(rows, value):
                T[rows, :] = third_coeff * M[rows, :] + fifth_coeff * value + jnp.where(
                    eye(rows.start), first_coeff, 0.0)
            multiply(M, M, poly)
            multiply(Q, T, put(U))
            Q[...] = U[...]

            @pl.when(k < NS_STEPS - 1)
            def _():
                multiply(M, T, put(U))
                multiply(T, U, put(M))
            return carry

        lax.fori_loop(0, NS_STEPS, ns_step, 0)

    def dual_step(first):
        multiply(B if first else F, Q, put(U))
        term = (dual_rate * -learn_rate) * (U[...] + U[...].T)
        L[...] = term if first else L[...] + term

    M[...] = A[...]
    orthogonalize()
    dual_step(True)
    for iteration in range(1, DUAL_ITERS):
        S[...] = 4.0 * L[...]
        F[...] = B[...]
        multiply(D, S, add(F))
        multiply(S, B, put(U))
        M[...] = A[...] + U[...].T
        multiply(S, F, add(M))
        orthogonalize()
        dual_step(False)
    send[0:size, :] = (Q[...] * (clip * -learn_rate)).astype(BF16)
    multiply(S, Q, put(U))
    send[size : 2 * size, :] = (U[...] * -learn_rate).astype(BF16)
    depth = size // n
    pair = r + 1 - 2 * lax.rem(r, 2)
    dual[...] = L[pl.ds(pl.multiple_of(r * depth, depth), depth), :]
    send[2 * size :, :] = L[pl.ds(pl.multiple_of(pair * depth, depth), depth), :].astype(BF16)


def on_device(key_weight, value_weight, key_grad, value_grad):
    layers, n = lax.axis_size("layer"), lax.axis_size("rows")
    kw, vw, kg, vg = (x.reshape(x.shape[1:]) for x in (key_weight, value_weight, key_grad, value_grad))
    rows, size = kw.shape
    nb = size // TILE
    chunks = 2 * nb + 1
    depth = size // n
    entries = 2.0 * rows * size * layers * n
    shape = jax.ShapeDtypeStruct
    packed = (chunks, TILE, size)
    limit = 48 * 1024 * 1024
    own, other, tile = pl.pallas_call(
        functools.partial(gram_kernel, nb),
        out_shape=(shape(packed, BF16), shape(packed, BF16), shape((8, TILE), F32)),
        in_specs=[VMEM] * 4,
        out_specs=(VMEM,) * 3,
        scratch_shapes=[pltpu.VMEM((size, rows), BF16)] * 2,
        compiler_params=pltpu.CompilerParams(vmem_limit_bytes=limit),
        name="grams",
    )(kw, vw, kg, vg)
    sums, total = pl.pallas_call(
        functools.partial(reduce_kernel, layers, n),
        out_shape=(shape(packed, F32), shape((8, TILE), F32)),
        in_specs=[VMEM] * 3,
        out_specs=(VMEM,) * 2,
        scratch_shapes=[pltpu.VMEM(packed, F32)]
        + [pltpu.VMEM(packed, BF16)] * 5
        + [
            pltpu.VMEM((layers - 1, 8, TILE), F32),
            pltpu.VMEM((8, TILE), F32),
            pltpu.VMEM((n - 1, 8, TILE), F32),
        ]
        + [pltpu.SemaphoreType.DMA((2, chunks))] * 3
        + [pltpu.SemaphoreType.DMA((2, layers - 1)), pltpu.SemaphoreType.DMA((2, n - 1))],
        compiler_params=pltpu.CompilerParams(
            collective_id=0, has_side_effects=True, vmem_limit_bytes=limit),
        name="reduce",
    )(own, other, tile)
    square = pltpu.VMEM((size, size), F32)
    send, dual = pl.pallas_call(
        functools.partial(dual_kernel, nb, n, entries),
        out_shape=(shape((2 * size + depth, size), BF16), shape((depth, size), F32)),
        in_specs=[VMEM] * 2,
        out_specs=(VMEM,) * 2,
        scratch_shapes=[square] * 10 + [pltpu.VMEM((size, size), BF16)] * 4,
        compiler_params=pltpu.CompilerParams(vmem_limit_bytes=limit),
        name="dual",
    )(sums, total)
    received = lax.ppermute(send, "rows", [(i, i + 1 - 2 * (i % 2)) for i in range(n)])
    even = lax.rem(lax.axis_index("rows"), 2) == 0
    received_dual = received[2 * size :].astype(F32)
    key_factor = jnp.where(even, send[: 2 * size], received[: 2 * size])
    value_factor = jnp.where(even, received[: 2 * size], send[: 2 * size])

    def update(g, w, factor):
        result = jnp.dot(g, factor[:size], preferred_element_type=F32)
        result = result + jnp.dot(w, factor[size:], preferred_element_type=F32)
        return result.astype(BF16)[None]

    return (
        update(kg, kw, key_factor),
        update(vg, vw, value_factor),
        jnp.where(even, dual, received_dual)[None],
        jnp.where(even, received_dual, dual)[None],
    )


def solution(mesh):
    placed = P("layer", "rows", None)
    return jax.shard_map(
        on_device,
        mesh=mesh,
        in_specs=(placed,) * 4,
        out_specs=(placed,) * 4,
        check_vma=False,
    )
```

```python
import functools

import jax
import jax.numpy as jnp
from jax import lax
from jax.experimental import pallas as pl
from jax.experimental.pallas import tpu as pltpu
from jax.sharding import PartitionSpec as P

DUAL_ITERS = 2
NS_STEPS = 3
first_coeff = 3.4445
third_coeff = -4.775
fifth_coeff = 2.0315
learn_rate = 0.1
dual_rate = 4.0
clip_target = 0.02
epsilon = 1e-06

TILE = 128
LAG = 2
AHEAD = 3
F32 = jnp.float32
BF16 = jnp.bfloat16
VMEM = pl.BlockSpec(memory_space=pltpu.VMEM)


def block_list(nb):
    upper = [(i, j) for i in range(nb) for j in range(i, nb)]
    return (
        [("A", i, j) for i, j in upper]
        + [("D", i, j) for i, j in upper]
        + [("B", i, j) for i in range(nb) for j in range(nb)]
    )


def strips(nb):
    runs, place = [], 0
    for name in ("A", "D"):
        for i in range(nb):
            runs.append((name, i, i, place))
            place += nb - i
    for i in range(nb):
        runs.append(("B", i, 0, place))
        place += nb
    return runs


def gram_kernel(nb, kw, vw, kg, vg, own, other, tile, gt, wt):
    parity = lax.rem(lax.axis_index("rows"), 2)

    def one(w, g, dst):
        gt[...] = g[...].T
        wt[...] = w[...].T
        for name, i, j, place in strips(nb):
            left = wt if name in ("D", "B") else gt
            right = w if name == "D" else g
            rows = left[i * TILE : (i + 1) * TILE, :]
            value = jnp.dot(rows, right[:, j * TILE :], preferred_element_type=F32).astype(BF16)
            for step in range(nb - j):
                chunk, column = divmod(place + step, nb)
                dst[chunk, :, column * TILE : (column + 1) * TILE] = value[
                    :, step * TILE : (step + 1) * TILE
                ]

    total = jnp.zeros((8, g_cols(kg)), F32)
    rows = kg.shape[0]
    for ref in (kg, vg):
        for start in range(0, rows, 128):
            part = ref[start : start + 128, :].astype(F32)
            total = total + jnp.sum((part * part).reshape(16, 8, -1), axis=0)
    folded = total[:, :TILE]
    for i in range(1, nb):
        folded = folded + total[:, i * TILE : (i + 1) * TILE]
    tile[...] = folded

    @pl.when(parity == 0)
    def _():
        one(vw, vg, other)
        one(kw, kg, own)

    @pl.when(parity == 1)
    def _():
        one(kw, kg, other)
        one(vw, vg, own)


def g_cols(ref):
    return ref.shape[-1]


def reduce_kernel(
    layers, n, wide, own, other, tile, out, total,
    acc, from_pair, from_left, from_right, to_left, to_right,
    wide_from_left, wide_from_right, wide_to_left, wide_to_right, passing,
    layer_tiles, tile_sum, row_tiles,
    pair_sems, left_sems, right_sems, layer_sems, row_sems,
):
    layer = lax.axis_index("layer")
    r = lax.axis_index("rows")
    m = n // 2
    c = r // 2
    pair = r + 1 - 2 * lax.rem(r, 2)
    chunks = own.shape[0]
    MESH = pl.DeviceIdType.MESH

    barrier = pltpu.get_barrier_semaphore()
    for o in range(1, layers):
        peer = (lax.rem(layer + o, layers), r)
        pl.semaphore_signal(barrier, inc=1, device_id=peer, device_id_type=MESH)
    for o in range(1, n):
        peer = (layer, lax.rem(r + o, n))
        pl.semaphore_signal(barrier, inc=1, device_id=peer, device_id_type=MESH)
    pl.semaphore_wait(barrier, layers - 1 + n - 1)

    def layer_copy(o):
        return pltpu.make_async_remote_copy(
            src_ref=tile, dst_ref=layer_tiles.at[o - 1],
            send_sem=layer_sems.at[0, o - 1], recv_sem=layer_sems.at[1, o - 1],
            device_id=(lax.rem(layer + o, layers), r), device_id_type=MESH)

    def row_copy(o):
        return pltpu.make_async_remote_copy(
            src_ref=tile_sum, dst_ref=row_tiles.at[o - 1],
            send_sem=row_sems.at[0, o - 1], recv_sem=row_sems.at[1, o - 1],
            device_id=(layer, lax.rem(r + o, n)), device_id_type=MESH)

    def pair_copy(k):
        return pltpu.make_async_remote_copy(
            src_ref=other.at[k], dst_ref=from_pair.at[k],
            send_sem=pair_sems.at[0, k], recv_sem=pair_sems.at[1, k],
            device_id=(layer, pair), device_id_type=MESH)

    def chain(src, dst, sems, offset):
        def copy(k):
            return pltpu.make_async_remote_copy(
                src_ref=src.at[k], dst_ref=dst.at[k],
                send_sem=sems.at[0, k], recv_sem=sems.at[1, k],
                device_id=(layer, lax.rem(r + offset, n)), device_id_type=MESH)
        return copy

    rights = [
        (wide_to_right, wide_from_left, chain(wide_to_right, wide_from_left, right_sems, 2)),
        (to_right, from_left, chain(to_right, from_left, right_sems, 2)),
    ]
    lefts = [
        (wide_to_left, wide_from_right, chain(wide_to_left, wide_from_right, left_sems, n - 2)),
        (to_left, from_right, chain(to_left, from_right, left_sems, n - 2)),
    ]

    def hop(k, kinds, first, last):
        for kind, (src, dst, copy) in enumerate(kinds):

            @pl.when((k < wide) if kind == 0 else (k >= wide))
            def _():
                passing[...] = acc[k]

                @pl.when(jnp.logical_not(first))
                def _():
                    copy(k).wait_recv()
                    arrived = dst[k].astype(F32)
                    out[k] = out[k] + arrived
                    passing[...] = passing[...] + arrived

                @pl.when(jnp.logical_not(last))
                def _():
                    src[k] = passing[...].astype(src.dtype)
                    copy(k).start()

    def hop_end(k, kinds, last):
        for kind, (src, dst, copy) in enumerate(kinds):

            @pl.when(((k < wide) if kind == 0 else (k >= wide)) & jnp.logical_not(last))
            def _():
                copy(k).wait_send()

    for o in range(1, layers):
        layer_copy(o).start()

    def begin(k, carry):
        pair_copy(k).start()
        return carry

    lax.fori_loop(0, AHEAD, begin, 0)
    for o in range(1, layers):
        layer_copy(o).wait_recv()
    value = tile[...]
    for o in range(1, layers):
        value = value + layer_tiles[o - 1]
    tile_sum[...] = value
    for o in range(1, n):
        row_copy(o).start()

    def step(t, carry):
        @pl.when(t + AHEAD < chunks)
        def _():
            pair_copy(t + AHEAD).start()

        @pl.when(t < chunks)
        def _():
            pair_copy(t).wait_recv()
            both = own[t].astype(F32) + from_pair[t].astype(F32)
            acc[t] = both
            out[t] = both

        k = t - LAG * c

        @pl.when((k >= 0) & (k < chunks))
        def _():
            hop(k, rights, c == 0, c == m - 1)

        q = t - LAG * (m - 1 - c)

        @pl.when((q >= 0) & (q < chunks))
        def _():
            hop(q, lefts, c == m - 1, c == 0)

        return carry

    lax.fori_loop(0, chunks + LAG * (m - 1), step, 0)

    for o in range(1, n):
        row_copy(o).wait_recv()
    value = tile_sum[...]
    for o in range(1, n):
        value = value + row_tiles[o - 1]
    total[...] = value

    def end(k, carry):
        pair_copy(k).wait_send()
        hop_end(k, rights, c == m - 1)
        hop_end(k, lefts, c == 0)
        return carry

    lax.fori_loop(0, chunks, end, 0)
    for o in range(1, layers):
        layer_copy(o).wait_send()
    for o in range(1, n):
        row_copy(o).wait_send()


def dual_kernel(nb, n, entries, packed, tile, send, dual, A, B, D, M, Q, T, L, S, F, U, h0, l0, h1, l1):
    size = nb * TILE
    half = size // 2
    r = lax.axis_index("rows")
    clip = clip_target * lax.rsqrt(jnp.full((1, TILE), jnp.sum(tile[...]) / entries + epsilon))
    clip = jnp.max(clip)

    for place, (name, i, j) in enumerate(block_list(nb)):
        chunk, column = divmod(place, nb)
        block = packed[chunk, :, column * TILE : (column + 1) * TILE]
        ref, scale = {"A": (A, clip * clip), "B": (B, clip), "D": (D, None)}[name]
        if scale is not None:
            block = block * scale
        ref[i * TILE : (i + 1) * TILE, j * TILE : (j + 1) * TILE] = block
        if name != "B" and i != j:
            ref[j * TILE : (j + 1) * TILE, i * TILE : (i + 1) * TILE] = block.T

    def split(ref, high, low):
        value = ref[...]
        scaled = value * 65537.0
        leading = scaled - (scaled - value)
        high[...] = leading.astype(BF16)
        low[...] = (value - leading).astype(BF16)

    def split_dot(start, xh, xl, yh, yl):
        rows = pl.ds(start, half)
        return (
            jnp.dot(xh[rows, :], yh[...], preferred_element_type=F32)
            + jnp.dot(xh[rows, :], yl[...], preferred_element_type=F32)
            + jnp.dot(xl[rows, :], yh[...], preferred_element_type=F32)
        )

    def multiply_rounded(x, y, store):
        h0[...] = x[...].astype(BF16)
        same = x is y
        if not same:
            h1[...] = y[...].astype(BF16)

        def body(i, carry):
            rows = pl.ds(pl.multiple_of(i * half, half), half)
            store(rows, jnp.dot(h0[rows, :], (h0 if same else h1)[...], preferred_element_type=F32))
            return carry

        lax.fori_loop(0, 2, body, 0)

    def multiply(x, y, store):
        split(x, h0, l0)
        same = x is y
        if not same:
            split(y, h1, l1)

        def body(i, carry):
            start = pl.multiple_of(i * half, half)
            store(pl.ds(start, half), split_dot(start, h0, l0, h0 if same else h1, l0 if same else l1))
            return carry

        lax.fori_loop(0, 2, body, 0)

    def eye(rows_start):
        a = lax.broadcasted_iota(jnp.int32, (half, size), 0) + rows_start
        b = lax.broadcasted_iota(jnp.int32, (half, size), 1)
        return a == b

    def put(ref):
        def store(rows, value):
            ref[rows, :] = value
        return store

    def add(ref):
        def store(rows, value):
            ref[rows, :] = ref[rows, :] + value
        return store

    def orthogonalize():
        squares = jnp.float32(0)
        for i in range(2):
            squares = squares + jnp.sum(
                jnp.where(eye(i * half), M[i * half : (i + 1) * half, :], 0.0))
        whole = jnp.full((1, size), squares + epsilon)
        M[...] = M[...] * (1.0 / whole)
        inverse = lax.rsqrt(whole)

        def ns_step(k, carry):
            def poly(rows, value):
                T[rows, :] = third_coeff * M[rows, :] + fifth_coeff * value + jnp.where(
                    eye(rows.start), first_coeff, 0.0)
            multiply_rounded(M, M, poly)

            @pl.when(k == 0)
            def _():
                Q[...] = T[...] * inverse

            @pl.when(k > 0)
            def _():
                multiply_rounded(Q, T, put(U))
                Q[...] = U[...]

            @pl.when(k == 0)
            def _():
                multiply(M, T, put(U))
                multiply(T, U, put(M))

            @pl.when((k > 0) & (k < NS_STEPS - 1))
            def _():
                multiply_rounded(M, T, put(U))
                multiply_rounded(T, U, put(M))
            return carry

        lax.fori_loop(0, NS_STEPS, ns_step, 0)

    def dual_step(first):
        multiply(B if first else F, Q, put(U))
        term = (dual_rate * -learn_rate) * (U[...] + U[...].T)
        L[...] = term if first else L[...] + term

    M[...] = A[...]
    orthogonalize()
    dual_step(True)
    for iteration in range(1, DUAL_ITERS):
        S[...] = 4.0 * L[...]
        F[...] = B[...]
        multiply_rounded(D, S, add(F))
        multiply_rounded(S, B, put(U))
        M[...] = A[...] + U[...].T
        multiply_rounded(S, F, add(M))
        orthogonalize()
        dual_step(False)
    send[0:size, :] = (Q[...] * (clip * -learn_rate)).astype(BF16)
    multiply_rounded(S, Q, put(U))
    send[size : 2 * size, :] = (U[...] * -learn_rate).astype(BF16)
    depth = size // n
    pair = r + 1 - 2 * lax.rem(r, 2)
    dual[...] = L[pl.ds(pl.multiple_of(r * depth, depth), depth), :]
    send[2 * size :, :] = L[pl.ds(pl.multiple_of(pair * depth, depth), depth), :].astype(BF16)


def on_device(key_weight, value_weight, key_grad, value_grad):
    layers, n = lax.axis_size("layer"), lax.axis_size("rows")
    kw, vw, kg, vg = (x.reshape(x.shape[1:]) for x in (key_weight, value_weight, key_grad, value_grad))
    rows, size = kw.shape
    nb = size // TILE
    chunks = 2 * nb + 1
    wide = -(-(nb + 1) // 2)
    depth = size // n
    entries = 2.0 * rows * size * layers * n
    shape = jax.ShapeDtypeStruct
    packed = (chunks, TILE, size)
    limit = 28 * 1024 * 1024
    own, other, tile = pl.pallas_call(
        functools.partial(gram_kernel, nb),
        out_shape=(shape(packed, BF16), shape(packed, BF16), shape((8, TILE), F32)),
        in_specs=[VMEM] * 4,
        out_specs=(VMEM,) * 3,
        scratch_shapes=[pltpu.VMEM((size, rows), BF16)] * 2,
        compiler_params=pltpu.CompilerParams(vmem_limit_bytes=limit),
        name="grams",
    )(kw, vw, kg, vg)
    sums, total = pl.pallas_call(
        functools.partial(reduce_kernel, layers, n, wide),
        out_shape=(shape(packed, F32), shape((8, TILE), F32)),
        in_specs=[VMEM] * 3,
        out_specs=(VMEM,) * 2,
        scratch_shapes=[pltpu.VMEM(packed, F32)]
        + [pltpu.VMEM(packed, BF16)] * 5
        + [pltpu.VMEM((wide,) + packed[1:], F32)] * 4
        + [pltpu.VMEM(packed[1:], F32)]
        + [
            pltpu.VMEM((layers - 1, 8, TILE), F32),
            pltpu.VMEM((8, TILE), F32),
            pltpu.VMEM((n - 1, 8, TILE), F32),
        ]
        + [pltpu.SemaphoreType.DMA((2, chunks))] * 3
        + [pltpu.SemaphoreType.DMA((2, layers - 1)), pltpu.SemaphoreType.DMA((2, n - 1))],
        compiler_params=pltpu.CompilerParams(
            collective_id=0, has_side_effects=True, vmem_limit_bytes=limit),
        name="reduce",
    )(own, other, tile)
    square = pltpu.VMEM((size, size), F32)
    send, dual = pl.pallas_call(
        functools.partial(dual_kernel, nb, n, entries),
        out_shape=(shape((2 * size + depth, size), BF16), shape((depth, size), F32)),
        in_specs=[VMEM] * 2,
        out_specs=(VMEM,) * 2,
        scratch_shapes=[square] * 10 + [pltpu.VMEM((size, size), BF16)] * 4,
        compiler_params=pltpu.CompilerParams(vmem_limit_bytes=limit),
        name="dual",
    )(sums, total)
    received = lax.ppermute(send, "rows", [(i, i + 1 - 2 * (i % 2)) for i in range(n)])
    even = lax.rem(lax.axis_index("rows"), 2) == 0
    received_dual = received[2 * size :].astype(F32)
    key_factor = jnp.where(even, send[: 2 * size], received[: 2 * size])
    value_factor = jnp.where(even, received[: 2 * size], send[: 2 * size])

    def update(g, w, factor):
        result = jnp.dot(g, factor[:size], preferred_element_type=F32)
        result = result + jnp.dot(w, factor[size:], preferred_element_type=F32)
        return result.astype(BF16)[None]

    return (
        update(kg, kw, key_factor),
        update(vg, vw, value_factor),
        jnp.where(even, dual, received_dual)[None],
        jnp.where(even, received_dual, dual)[None],
    )


def solution(mesh):
    placed = P("layer", "rows", None)
    return jax.shard_map(
        on_device,
        mesh=mesh,
        in_specs=(placed,) * 4,
        out_specs=(placed,) * 4,
        check_vma=False,
    )
```
